32 devices in a mesh: ja: 2 (over x), ka: 4 (over z), ia: 4 (over y, core).
Axes of the slice: x: 2, y: 2, z: 4, core: 2. Of those that a mesh axis runs over, the one named last changes fastest.
Arguments:
- tensor: float32 [48, 1024, 2048], P('ia', 'ja', 'ka'), may hold values from -6 to 6
- factor_b: float32 [1024, 256], P(('ja', 'ka', 'ia')), may hold values from -0.9 to 0.9, as said below
- factor_c: float32 [2048, 256], P(('ka', 'ja', 'ia')), may hold values from -0.9 to 0.9, as said below
Outputs:
- new_factor: float32 [48, 256], P('ia')
The draws below stay inside these ranges and needn't reach their ends.
Inputs may be any that keep to these rules, and one draw needn't show every extreme that they name: `factor_b`: real entries of the factor. `factor_c`: real entries of the factor.
All inputs are finite; a program needn't handle non-finite values.
Results may differ from the reference program's by a relative error of at most 0.000086.
Values sent between devices are 32-bit elements; how exact they have to be, the bound alone decides.
A program may use at most 64 MiB of HBM per device.

```python
import jax
import jax.numpy as jnp
from jax import lax

R = 256
I = 48
J = 1024
K = 2048


def factor_values(key, length, width):
    first, second, third = jax.random.split(key, 3)
    entries = jnp.clip(jax.random.normal(first, (length, width), jnp.float32), -5.0, 5.0)
    common = jnp.clip(jax.random.normal(second, (length, 1), jnp.float32), -5.0, 5.0)
    trend = jnp.exp(jnp.log(3.0) * jnp.arange(length, dtype=jnp.float32) / length)
    spread = jnp.exp(jax.random.uniform(third, (length, 1), jnp.float32) * jnp.log(3.0))
    values = (entries + 0.5 * common) * trend[:, None] * spread / (4.0 * jnp.sqrt(jnp.float32(length)))
    return jnp.clip(values, -0.9, 0.9)


def draw_factor_b(key, part):
    return factor_values(jax.random.fold_in(key, 11), J, R)


def draw_factor_c(key, part):
    return factor_values(jax.random.fold_in(key, 23), K, R)


def steps_of(rng, shape, cuts, smallest, high):
    loudness, own = 1.0, jax.random.fold_in(rng, 6)
    for axis_at, blocks in cuts:
        heights = jnp.exp(jax.random.uniform(jax.random.fold_in(own, axis_at), (blocks,), jnp.float32, smallest / len(cuts), high / len(cuts)))
        loudness = loudness * jnp.repeat(heights, shape[axis_at] // blocks).reshape([-1 if axis == axis_at else 1 for axis in range(len(shape))])
    return loudness


def centred(stream_key, dims, scale, most, pieces=(), kind=jnp.bfloat16):
    array = jax.random.normal(stream_key, dims, jnp.float32) * scale
    if len(pieces) > 0:
        array = steps_of(stream_key, dims, pieces, -0.22, 0.18) * array
    return jnp.clip(array, min=-most, max=most).astype(kind)


def setup_inputs(seed: int = 0) -> dict:
    key_list = jax.random.split(jax.random.key(seed), 4)
    return {
        "tensor": centred(key_list[0], (I, J, K), 1.0, 6.0, ((0, 4), (1, 2), (2, 4)), jnp.float32),
        "factor_b": draw_factor_b(jax.random.fold_in(key_list[3], 71), 0),
        "factor_c": draw_factor_c(jax.random.fold_in(key_list[3], 71), 0),
    }


exact_mode = lax.Precision.HIGHEST

def upper_of(matrix):
    gram = jnp.dot(matrix.T.astype(jnp.float32), matrix.astype(jnp.float32), precision=exact_mode, preferred_element_type=jnp.float32)
    return jnp.linalg.cholesky(gram).T

def square_of(upper):
    return jnp.dot(upper.T.astype(jnp.float32), upper.astype(jnp.float32), precision=exact_mode, preferred_element_type=jnp.float32)

def reference(tensor, factor_b, factor_c):
    upper_b = upper_of(factor_b)
    upper_c = upper_of(factor_c)
    normal = square_of(upper_b) * square_of(upper_c)

    def one_slice(matrix):
        section = jnp.dot(matrix.astype(jnp.float32), factor_c.astype(jnp.float32), precision=exact_mode, preferred_element_type=jnp.float32)
        return jnp.sum(section * factor_b, axis=0)
    product = lax.map(one_slice, tensor)
    lower_factor = jnp.linalg.cholesky(normal)
    halfway = lax.linalg.triangular_solve(lower_factor, product.T, left_side=True, lower=True)
    solved = lax.linalg.triangular_solve(lower_factor, halfway, left_side=True, lower=True, transpose_a=True)
    return solved.T
```

```python
import functools

import jax
import jax.numpy as jnp
from jax import lax
from jax.experimental import pallas as pl
from jax.experimental.pallas import tpu as pltpu
from jax.sharding import PartitionSpec as P

exact_mode = lax.Precision.HIGHEST
tile_rows = 8


def bits_of(count):
    found, bit = [], count // 2
    while bit >= 1:
        found.append(bit)
        bit //= 2
    return found


def flip(index, bit):
    return index + bit * (1 - 2 * ((index // bit) % 2))


def flip_mask(index, mask):
    bit = 1
    while bit <= mask:
        if mask & bit:
            index = flip(index, bit)
        bit *= 2
    return index


def exact_dot(a, b, dims):
    return lax.dot_general(
        a, b, (dims, ((), ())), precision=exact_mode, preferred_element_type=jnp.float32
    )


class Gather:
    def __init__(self, buffer, send_sems, recv_sems, position, links):
        self.buffer, self.send_sems, self.recv_sems = buffer, send_sems, recv_sems
        self.position, self.links = position, links
        self.sends = []

    def forward(self, mask):
        low = mask & -mask
        chunk = flip_mask(self.position, mask)
        for bit, device in self.links:
            if mask == 0 or bit < low:
                copy = pltpu.make_async_remote_copy(
                    src_ref=self.buffer.at[chunk],
                    dst_ref=self.buffer.at[chunk],
                    send_sem=self.send_sems.at[mask | bit],
                    recv_sem=self.recv_sems.at[mask | bit],
                    device_id=device,
                    device_id_type=pl.DeviceIdType.MESH,
                )
                copy.start()
                self.sends.append(copy)

    def arrive(self, mask):
        low = mask & -mask
        chunk = flip_mask(self.position, mask)
        device = [d for bit, d in self.links if bit == low][0]
        pltpu.make_async_remote_copy(
            src_ref=self.buffer.at[chunk],
            dst_ref=self.buffer.at[chunk],
            send_sem=self.send_sems.at[mask],
            recv_sem=self.recv_sems.at[mask],
            device_id=device,
            device_id_type=pl.DeviceIdType.MESH,
        ).wait_recv()

    def masks(self):
        count = 2 ** len(self.links)
        return sorted(range(1, count), key=lambda m: (bin(m).count("1"), -m))

    def finish(self):
        for copy in self.sends:
            copy.wait_send()


def exchange_kernel(
    names,
    sizes,
    tensor_ref,
    b_ref,
    c_ref,
    normal_ref,
    product_ref,
    t_buf,
    b_buf,
    c_buf,
    n_buf,
    gram_b,
    gram_c,
    b_in,
    c_in,
    p_in,
    c_high,
    c_low,
    b_flat,
    p_buf,
    t_sem,
    b_send,
    b_recv,
    c_send,
    c_recv,
    n_send,
    n_recv,
    gb_sem,
    gc_sem,
    p_sem,
):
    slab_rows = tensor_ref.shape[0]
    width = b_ref.shape[1]
    at = {name: lax.axis_index(name) for name in names}

    def partner(name, bit):
        return tuple(flip(at[n], bit) if n == name else at[n] for n in names)

    def fetch(i):
        return pltpu.make_async_copy(tensor_ref.at[i], t_buf.at[i], t_sem.at[i])

    for i in range(slab_rows):
        fetch(i).start()

    partners = [partner(n, bit) for n in names for bit in bits_of(sizes[n])]
    barrier = pltpu.get_barrier_semaphore()
    for device in partners:
        pl.semaphore_signal(barrier, inc=1, device_id=device, device_id_type=pl.DeviceIdType.MESH)

    ia_links = [(bit, partner("ia", bit)) for bit in bits_of(sizes["ia"])]
    c_links = [(bit * sizes["ia"], partner("ja", bit)) for bit in bits_of(sizes["ja"])] + ia_links
    b_links = [(bit * sizes["ia"], partner("ka", bit)) for bit in bits_of(sizes["ka"])] + ia_links
    c_at = at["ja"] * sizes["ia"] + at["ia"]
    b_at = at["ka"] * sizes["ia"] + at["ia"]
    c_buf[c_at] = c_ref[...]
    b_buf[b_at] = b_ref[...]
    pl.semaphore_wait(barrier, len(partners))

    c_all = Gather(c_buf, c_send, c_recv, c_at, c_links)
    b_all = Gather(b_buf, b_send, b_recv, b_at, b_links)
    c_all.forward(0)
    b_all.forward(0)
    for mask in c_all.masks():
        c_all.arrive(mask)
        c_all.forward(mask)

    deep = c_buf.shape[0] * c_buf.shape[1]
    whole_c = c_buf[...].reshape(deep, width)
    high = whole_c.astype(jnp.bfloat16)
    c_high[...] = high
    c_low[...] = (whole_c - high.astype(jnp.float32)).astype(jnp.bfloat16)
    gram_c[...] = exact_dot(whole_c, whole_c, ((0,), (0,)))

    slab = width // sizes["ia"]
    rows = pl.ds(pl.multiple_of(at["ia"] * slab, slab), slab)

    def stage(buffer, inbox, sems, step, device):
        return pltpu.make_async_remote_copy(
            src_ref=buffer,
            dst_ref=inbox.at[step],
            send_sem=sems.at[0, step],
            recv_sem=sems.at[1, step],
            device_id=device,
            device_id_type=pl.DeviceIdType.MESH,
        )

    ka_partners = [partner("ka", bit) for bit in bits_of(sizes["ka"])]
    ja_partners = [partner("ja", bit) for bit in bits_of(sizes["ja"])]
    c_steps = [stage(gram_c.at[rows], c_in, gc_sem, s, d) for s, d in enumerate(ka_partners)]
    b_steps = [stage(gram_b.at[rows], b_in, gb_sem, s, d) for s, d in enumerate(ja_partners)]
    c_steps[0].start()

    for mask in b_all.masks():
        b_all.arrive(mask)
        b_all.forward(mask)
    whole_b = b_buf[...].reshape(b_buf.shape[0] * b_buf.shape[1], width)
    b_flat[...] = whole_b
    gram_b[...] = exact_dot(whole_b, whole_b, ((0,), (0,)))
    b_steps[0].start()

    def rows_of_product(first, last):
        def one(i, carry):
            fetch(i).wait()
            block = t_buf[i]
            block_high = block.astype(jnp.bfloat16)
            block_low = (block - block_high.astype(jnp.float32)).astype(jnp.bfloat16)
            dims = ((1,), (0,))

            def pass_of(left, right):
                return lax.dot_general(
                    left, right, (dims, ((), ())), preferred_element_type=jnp.float32
                )

            section = (
                pass_of(block_low, c_high[...])
                + pass_of(block_high, c_low[...])
                + pass_of(block_high, c_high[...])
            )
            p_buf[pl.ds(i, 1), :] = jnp.sum(section * b_flat[...], axis=0, keepdims=True)
            return carry

        lax.fori_loop(first, last, one, 0)

    pending = [("c", s) for s in range(len(c_steps))] + [("b", s) for s in range(len(b_steps))]
    parts = len(pending) + 1
    cuts = [slab_rows * p // parts for p in range(parts + 1)]
    for part, (kind, step) in enumerate(pending):
        rows_of_product(cuts[part], cuts[part + 1])
        steps, buffer, inbox = (
            (c_steps, gram_c, c_in) if kind == "c" else (b_steps, gram_b, b_in)
        )
        steps[step].wait()
        buffer[rows, :] += inbox[step]
        if step + 1 < len(steps):
            steps[step + 1].start()

    n_buf[at["ia"]] = gram_b[rows, :] * gram_c[rows, :]
    n_all = Gather(n_buf, n_send, n_recv, at["ia"], ia_links)
    n_all.forward(0)
    rows_of_product(cuts[parts - 1], cuts[parts])
    p_steps = [stage(p_buf, p_in, p_sem, s, d) for s, d in enumerate(ja_partners + ka_partners)]
    p_steps[0].start()
    for mask in n_all.masks():
        n_all.arrive(mask)
        n_all.forward(mask)
    normal_ref[...] = n_buf[...].reshape(width, width)
    for step, copy in enumerate(p_steps):
        copy.wait()
        p_buf[...] += p_in[step]
        if step + 1 < len(p_steps):
            p_steps[step + 1].start()
    product_ref[...] = p_buf[...]
    n_all.finish()
    b_all.finish()
    c_all.finish()


def inverse_of(matrix):
    size = matrix.shape[0]
    count = size // tile_rows
    blocks = [matrix[tile_rows * i : tile_rows * (i + 1), :] for i in range(count)]
    lane = lax.broadcasted_iota(jnp.int32, (tile_rows, size), 1)
    row = lax.broadcasted_iota(jnp.int32, (tile_rows, size), 0)
    full = (tile_rows, size)
    for b in range(count):
        start = tile_rows * b
        inside = (lane >= start) & (lane < start + tile_rows)
        own = [
            jnp.broadcast_to(blocks[b][:, start + j : start + j + 1], full)
            for j in range(tile_rows)
        ]
        panel = jnp.where(inside, jnp.where(lane - start == row, 1.0, 0.0), blocks[b])
        for j in range(tile_rows):
            scale = 1.0 / jnp.broadcast_to(own[j][j : j + 1, :], full)
            here = row == j
            factor = jnp.where(here, 0.0, own[j])
            for c in range(j + 1, tile_rows):
                line = jnp.broadcast_to(own[c][j : j + 1, :], full) * scale
                own[c] = jnp.where(here, line, own[c] - factor * line)
            line = jnp.broadcast_to(panel[j : j + 1, :], full) * scale
            panel = jnp.where(here, line, panel - factor * line)
        lines = [jnp.broadcast_to(panel[j : j + 1, :], full) for j in range(tile_rows)]
        for i in range(count):
            if i == b:
                continue
            new = jnp.where(inside, 0.0, blocks[i])
            for j in range(tile_rows):
                new = new - jnp.broadcast_to(blocks[i][:, start + j : start + j + 1], full) * lines[j]
            blocks[i] = new
        blocks[b] = panel
    return jnp.concatenate(blocks, axis=0)


def solve_kernel(normal_ref, product_ref, out_ref):
    half = normal_ref.shape[0] // 2
    plain, turned = ((1,), (0,)), ((1,), (1,))
    corner = inverse_of(normal_ref[:half, :half])
    below = normal_ref[half:, :half]
    weight = exact_dot(below, corner, plain)
    rest = inverse_of(normal_ref[half:, half:] - exact_dot(weight, below, turned))
    left, right = product_ref[:, :half], product_ref[:, half:]
    second = exact_dot(right - exact_dot(left, weight, turned), rest, plain)
    out_ref[:, half:] = second
    out_ref[:, :half] = exact_dot(left - exact_dot(second, below, plain), corner, plain)


def shards(names, sizes, tensor, factor_b, factor_c):
    slab_rows, mode_two, mode_three = tensor.shape
    width = factor_b.shape[1]
    b_chunks, c_chunks = sizes["ka"] * sizes["ia"], sizes["ja"] * sizes["ia"]
    ka_steps, ja_steps = len(bits_of(sizes["ka"])), len(bits_of(sizes["ja"]))
    slab = width // sizes["ia"]
    f32, bf16 = jnp.float32, jnp.bfloat16
    vmem = pl.BlockSpec(memory_space=pltpu.VMEM)
    dma = pltpu.SemaphoreType.DMA
    normal, product = pl.pallas_call(
        functools.partial(exchange_kernel, names, sizes),
        out_shape=(
            jax.ShapeDtypeStruct((width, width), f32),
            jax.ShapeDtypeStruct((slab_rows, width), f32),
        ),
        in_specs=[pl.BlockSpec(memory_space=pl.ANY), vmem, vmem],
        out_specs=(vmem, vmem),
        scratch_shapes=[
            pltpu.VMEM(tensor.shape, f32),
            pltpu.VMEM((b_chunks,) + factor_b.shape, f32),
            pltpu.VMEM((c_chunks,) + factor_c.shape, f32),
            pltpu.VMEM((sizes["ia"], slab, width), f32),
            pltpu.VMEM((width, width), f32),
            pltpu.VMEM((width, width), f32),
            pltpu.VMEM((ja_steps, slab, width), f32),
            pltpu.VMEM((ka_steps, slab, width), f32),
            pltpu.VMEM((ja_steps + ka_steps, slab_rows, width), f32),
            pltpu.VMEM((mode_three, width), bf16),
            pltpu.VMEM((mode_three, width), bf16),
            pltpu.VMEM((mode_two, width), f32),
            pltpu.VMEM((slab_rows, width), f32),
            dma((slab_rows,)),
            dma((b_chunks,)),
            dma((b_chunks,)),
            dma((c_chunks,)),
            dma((c_chunks,)),
            dma((sizes["ia"],)),
            dma((sizes["ia"],)),
            dma((2, ja_steps)),
            dma((2, ka_steps)),
            dma((2, ja_steps + ka_steps)),
        ],
        compiler_params=pltpu.CompilerParams(
            collective_id=0, has_side_effects=True, vmem_limit_bytes=40 * 2**20
        ),
        name="exchange",
    )(tensor, factor_b, factor_c)
    return pl.pallas_call(
        solve_kernel,
        out_shape=jax.ShapeDtypeStruct((slab_rows, width), f32),
        in_specs=[vmem, vmem],
        out_specs=vmem,
        compiler_params=pltpu.CompilerParams(vmem_limit_bytes=16 * 2**20),
        name="solve",
    )(normal, product)


def solution(mesh):
    names = tuple(mesh.axis_names)
    sizes = {name: mesh.shape[name] for name in names}
    return jax.shard_map(
        functools.partial(shards, names, sizes),
        mesh=mesh,
        in_specs=(P("ia", "ja", "ka"), P(("ja", "ka", "ia"), None), P(("ka", "ja", "ia"), None)),
        out_specs=P("ia", None),
        check_vma=False,
    )
```

```python
import functools

import jax
import jax.numpy as jnp
from jax import lax
from jax.experimental import pallas as pl
from jax.experimental.pallas import tpu as pltpu
from jax.sharding import PartitionSpec as P

exact_mode = lax.Precision.HIGHEST
tile_rows = 8


def bits_of(count):
    found, bit = [], count // 2
    while bit >= 1:
        found.append(bit)
        bit //= 2
    return found


def flip(index, bit):
    return index + bit * (1 - 2 * ((index // bit) % 2))


def flip_mask(index, mask):
    bit = 1
    while bit <= mask:
        if mask & bit:
            index = flip(index, bit)
        bit *= 2
    return index


def exact_dot(a, b, dims):
    return lax.dot_general(
        a, b, (dims, ((), ())), precision=exact_mode, preferred_element_type=jnp.float32
    )


class Gather:
    def __init__(self, buffer, send_sems, recv_sems, position, links):
        self.buffer, self.send_sems, self.recv_sems = buffer, send_sems, recv_sems
        self.position, self.links = position, links
        self.sends = []

    def forward(self, mask):
        low = mask & -mask
        chunk = flip_mask(self.position, mask)
        for bit, device in self.links:
            if mask == 0 or bit < low:
                copy = pltpu.make_async_remote_copy(
                    src_ref=self.buffer.at[chunk],
                    dst_ref=self.buffer.at[chunk],
                    send_sem=self.send_sems.at[mask | bit],
                    recv_sem=self.recv_sems.at[mask | bit],
                    device_id=device,
                    device_id_type=pl.DeviceIdType.MESH,
                )
                copy.start()
                self.sends.append(copy)

    def arrive(self, mask):
        low = mask & -mask
        chunk = flip_mask(self.position, mask)
        device = [d for bit, d in self.links if bit == low][0]
        pltpu.make_async_remote_copy(
            src_ref=self.buffer.at[chunk],
            dst_ref=self.buffer.at[chunk],
            send_sem=self.send_sems.at[mask],
            recv_sem=self.recv_sems.at[mask],
            device_id=device,
            device_id_type=pl.DeviceIdType.MESH,
        ).wait_recv()

    def masks(self):
        count = 2 ** len(self.links)
        return sorted(range(1, count), key=lambda m: (bin(m).count("1"), -m))

    def finish(self):
        for copy in self.sends:
            copy.wait_send()


def exchange_kernel(
    names,
    sizes,
    tensor_ref,
    b_ref,
    c_ref,
    normal_ref,
    product_ref,
    t_buf,
    b_buf,
    c_buf,
    n_buf,
    gram_b,
    gram_c,
    b_in,
    c_in,
    p_in,
    c_split,
    b_flat,
    p_buf,
    t_sem,
    b_send,
    b_recv,
    c_send,
    c_recv,
    n_send,
    n_recv,
    gb_sem,
    gc_sem,
    p_sem,
    own_sem,
):
    slab_rows = tensor_ref.shape[0]
    width = b_ref.shape[1]
    at = {name: lax.axis_index(name) for name in names}

    def partner(name, bit):
        return tuple(flip(at[n], bit) if n == name else at[n] for n in names)

    def fetch(i):
        return pltpu.make_async_copy(tensor_ref.at[i], t_buf.at[i], t_sem.at[i])

    partners = [partner(n, bit) for n in names for bit in bits_of(sizes[n])]
    barrier = pltpu.get_barrier_semaphore()
    for device in partners:
        pl.semaphore_signal(barrier, inc=1, device_id=device, device_id_type=pl.DeviceIdType.MESH)

    ia_links = [(bit, partner("ia", bit)) for bit in bits_of(sizes["ia"])]
    c_links = [(bit * sizes["ia"], partner("ja", bit)) for bit in bits_of(sizes["ja"])] + ia_links
    b_links = [(bit * sizes["ia"], partner("ka", bit)) for bit in bits_of(sizes["ka"])] + ia_links
    c_at = at["ja"] * sizes["ia"] + at["ia"]
    b_at = at["ka"] * sizes["ia"] + at["ia"]
    own_c = pltpu.make_async_copy(c_ref, c_buf.at[c_at], own_sem.at[0])
    own_b = pltpu.make_async_copy(b_ref, b_buf.at[b_at], own_sem.at[1])
    own_c.start()
    own_b.start()
    for i in range(slab_rows):
        fetch(i).start()
    own_c.wait()
    own_b.wait()
    pl.semaphore_wait(barrier, len(partners))

    c_all = Gather(c_buf, c_send, c_recv, c_at, c_links)
    b_all = Gather(b_buf, b_send, b_recv, b_at, b_links)
    c_all.forward(0)
    b_all.forward(0)
    arrivals = [(bin(m).count("1"), 0, k, c_all, m) for k, m in enumerate(c_all.masks())]
    arrivals += [(bin(m).count("1"), 1, k, b_all, m) for k, m in enumerate(b_all.masks())]
    for _, _, _, gather, mask in sorted(arrivals, key=lambda a: a[:3]):
        gather.arrive(mask)
        gather.forward(mask)

    deep = c_buf.shape[0] * c_buf.shape[1]
    whole_c = c_buf[...].reshape(deep, width)
    high = whole_c.astype(jnp.bfloat16)
    c_split[:deep] = high
    c_split[deep : 2 * deep] = (whole_c - high.astype(jnp.float32)).astype(jnp.bfloat16)
    c_split[2 * deep :] = high
    gram_c[...] = exact_dot(whole_c, whole_c, ((0,), (0,)))

    slab = width // sizes["ia"]
    rows = pl.ds(pl.multiple_of(at["ia"] * slab, slab), slab)

    def stage(buffer, inbox, sems, step, device):
        return pltpu.make_async_remote_copy(
            src_ref=buffer,
            dst_ref=inbox.at[step],
            send_sem=sems.at[0, step],
            recv_sem=sems.at[1, step],
            device_id=device,
            device_id_type=pl.DeviceIdType.MESH,
        )

    ka_partners = [partner("ka", bit) for bit in bits_of(sizes["ka"])]
    ja_partners = [partner("ja", bit) for bit in bits_of(sizes["ja"])]
    c_steps = [stage(gram_c.at[rows], c_in, gc_sem, s, d) for s, d in enumerate(ka_partners)]
    b_steps = [stage(gram_b.at[rows], b_in, gb_sem, s, d) for s, d in enumerate(ja_partners)]
    c_steps[0].start()

    whole_b = b_buf[...].reshape(b_buf.shape[0] * b_buf.shape[1], width)
    b_flat[...] = whole_b
    gram_b[...] = exact_dot(whole_b, whole_b, ((0,), (0,)))
    b_steps[0].start()

    def rows_of_product(first, last):
        def one(i, carry):
            fetch(i).wait()
            block = t_buf[i]
            block_high = block.astype(jnp.bfloat16)
            block_low = (block - block_high.astype(jnp.float32)).astype(jnp.bfloat16)
            section = jnp.dot(
                jnp.concatenate([block_low, block_high, block_high], axis=1),
                c_split[...],
                preferred_element_type=jnp.float32,
            )
            p_buf[pl.ds(i, 1), :] = jnp.sum(section * b_flat[...], axis=0, keepdims=True)
            return carry

        lax.fori_loop(first, last, one, 0)

    pending = [("c", s) for s in range(len(c_steps))] + [("b", s) for s in range(len(b_steps))]
    pending.sort(key=lambda p: p[1])
    parts = len(pending)
    cuts = [slab_rows * p // parts for p in range(parts + 1)]
    for part, (kind, step) in enumerate(pending):
        rows_of_product(cuts[part], cuts[part + 1])
        steps, buffer, inbox = (
            (c_steps, gram_c, c_in) if kind == "c" else (b_steps, gram_b, b_in)
        )
        steps[step].wait()
        buffer[rows, :] += inbox[step]
        if step + 1 < len(steps):
            steps[step + 1].start()

    n_buf[at["ia"]] = gram_b[rows, :] * gram_c[rows, :]
    n_all = Gather(n_buf, n_send, n_recv, at["ia"], ia_links)
    n_all.forward(0)
    p_steps = [stage(p_buf, p_in, p_sem, s, d) for s, d in enumerate(ja_partners + ka_partners)]
    p_steps[0].start()
    masks = n_all.masks()
    for step, copy in enumerate(p_steps):
        copy.wait()
        p_buf[...] += p_in[step]
        if step + 1 < len(p_steps):
            p_steps[step + 1].start()
        for mask in masks:
            if bin(mask).count("1") == step + 1:
                n_all.arrive(mask)
                n_all.forward(mask)
    for mask in masks:
        if bin(mask).count("1") > len(p_steps):
            n_all.arrive(mask)
            n_all.forward(mask)
    normal_ref[...] = n_buf[...].reshape(width, width)
    product_ref[...] = p_buf[...]
    n_all.finish()
    b_all.finish()
    c_all.finish()


def inverse_of(matrix):
    size = matrix.shape[0]
    count = size // tile_rows
    blocks = [matrix[tile_rows * i : tile_rows * (i + 1), :] for i in range(count)]
    lane = lax.broadcasted_iota(jnp.int32, (tile_rows, size), 1)
    row = lax.broadcasted_iota(jnp.int32, (tile_rows, size), 0)
    full = (tile_rows, size)
    for b in range(count):
        start = tile_rows * b
        inside = (lane >= start) & (lane < start + tile_rows)
        own = [
            jnp.broadcast_to(blocks[b][:, start + j : start + j + 1], full)
            for j in range(tile_rows)
        ]
        panel = jnp.where(inside, jnp.where(lane - start == row, 1.0, 0.0), blocks[b])
        for j in range(tile_rows):
            scale = 1.0 / jnp.broadcast_to(own[j][j : j + 1, :], full)
            here = row == j
            factor = jnp.where(here, 0.0, own[j])
            for c in range(j + 1, tile_rows):
                line = jnp.broadcast_to(own[c][j : j + 1, :], full) * scale
                own[c] = jnp.where(here, line, own[c] - factor * line)
            line = jnp.broadcast_to(panel[j : j + 1, :], full) * scale
            panel = jnp.where(here, line, panel - factor * line)
        lines = [jnp.broadcast_to(panel[j : j + 1, :], full) for j in range(tile_rows)]
        for i in range(count):
            if i == b:
                continue
            new = jnp.where(inside, 0.0, blocks[i])
            for j in range(tile_rows):
                new = new - jnp.broadcast_to(blocks[i][:, start + j : start + j + 1], full) * lines[j]
            blocks[i] = new
        blocks[b] = panel
    return jnp.concatenate(blocks, axis=0)


def solve_kernel(normal_ref, product_ref, out_ref):
    half = normal_ref.shape[0] // 2
    plain, turned = ((1,), (0,)), ((1,), (1,))
    corner = inverse_of(normal_ref[:half, :half])
    below = normal_ref[half:, :half]
    weight = exact_dot(below, corner, plain)
    rest = inverse_of(normal_ref[half:, half:] - exact_dot(weight, below, turned))
    left, right = product_ref[:, :half], product_ref[:, half:]
    second = exact_dot(right - exact_dot(left, weight, turned), rest, plain)
    out_ref[:, half:] = second
    out_ref[:, :half] = exact_dot(left - exact_dot(second, below, plain), corner, plain)


def shards(names, sizes, tensor, factor_b, factor_c):
    slab_rows, mode_two, mode_three = tensor.shape
    width = factor_b.shape[1]
    b_chunks, c_chunks = sizes["ka"] * sizes["ia"], sizes["ja"] * sizes["ia"]
    ka_steps, ja_steps = len(bits_of(sizes["ka"])), len(bits_of(sizes["ja"]))
    slab = width // sizes["ia"]
    f32, bf16 = jnp.float32, jnp.bfloat16
    vmem = pl.BlockSpec(memory_space=pltpu.VMEM)
    dma = pltpu.SemaphoreType.DMA
    normal, product = pl.pallas_call(
        functools.partial(exchange_kernel, names, sizes),
        out_shape=(
            jax.ShapeDtypeStruct((width, width), f32),
            jax.ShapeDtypeStruct((slab_rows, width), f32),
        ),
        in_specs=[pl.BlockSpec(memory_space=pltpu.HBM)] * 3,
        out_specs=(vmem, vmem),
        scratch_shapes=[
            pltpu.VMEM(tensor.shape, f32),
            pltpu.VMEM((b_chunks,) + factor_b.shape, f32),
            pltpu.VMEM((c_chunks,) + factor_c.shape, f32),
            pltpu.VMEM((sizes["ia"], slab, width), f32),
            pltpu.VMEM((width, width), f32),
            pltpu.VMEM((width, width), f32),
            pltpu.VMEM((ja_steps, slab, width), f32),
            pltpu.VMEM((ka_steps, slab, width), f32),
            pltpu.VMEM((ja_steps + ka_steps, slab_rows, width), f32),
            pltpu.VMEM((3 * mode_three, width), bf16),
            pltpu.VMEM((mode_two, width), f32),
            pltpu.VMEM((slab_rows, width), f32),
            dma((slab_rows,)),
            dma((b_chunks,)),
            dma((b_chunks,)),
            dma((c_chunks,)),
            dma((c_chunks,)),
            dma((sizes["ia"],)),
            dma((sizes["ia"],)),
            dma((2, ja_steps)),
            dma((2, ka_steps)),
            dma((2, ja_steps + ka_steps)),
            dma((2,)),
        ],
        compiler_params=pltpu.CompilerParams(
            collective_id=0, has_side_effects=True, vmem_limit_bytes=40 * 2**20
        ),
        name="exchange",
    )(tensor, factor_b, factor_c)
    return pl.pallas_call(
        solve_kernel,
        out_shape=jax.ShapeDtypeStruct((slab_rows, width), f32),
        in_specs=[vmem, vmem],
        out_specs=vmem,
        compiler_params=pltpu.CompilerParams(vmem_limit_bytes=16 * 2**20),
        name="solve",
    )(normal, product)


def solution(mesh):
    names = tuple(mesh.axis_names)
    sizes = {name: mesh.shape[name] for name in names}
    return jax.shard_map(
        functools.partial(shards, names, sizes),
        mesh=mesh,
        in_specs=(P("ia", "ja", "ka"), P(("ja", "ka", "ia"), None), P(("ka", "ja", "ia"), None)),
        out_specs=P("ia", None),
        check_vma=False,
    )
```

```python
import functools

import jax
import jax.numpy as jnp
from jax import lax
from jax.experimental import pallas as pl
from jax.experimental.pallas import tpu as pltpu
from jax.sharding import PartitionSpec as P

exact_mode = lax.Precision.HIGHEST
tile_rows = 8
direct_ja, direct_ka, direct_ia, direct_n, direct_sums = True, True, False, True, True


def bits_of(count):
    found, bit = [], count // 2
    while bit >= 1:
        found.append(bit)
        bit //= 2
    return found


def flip(index, bit):
    return index + bit * (1 - 2 * ((index // bit) % 2))


def flip_mask(index, mask):
    bit = 1
    while bit <= mask:
        if mask & bit:
            index = flip(index, bit)
        bit *= 2
    return index


def exact_dot(a, b, dims):
    return lax.dot_general(
        a, b, (dims, ((), ())), precision=exact_mode, preferred_element_type=jnp.float32
    )


def combinations_of(bits):
    found = [0]
    for bit in bits:
        found += [mask | bit for mask in found]
    return found[1:]


class Gather:
    def __init__(self, buffer, send_sems, recv_sems, position, levels):
        self.buffer, self.send_sems, self.recv_sems = buffer, send_sems, recv_sems
        self.position, self.levels = position, levels
        self.sends = []
        self.order = [(0, -1, 0)]
        for number, level in enumerate(levels):
            self.order += [
                (depth + 1, number, mask | step)
                for depth, _, mask in self.order
                for step in level
            ]
        self.order = sorted(self.order[1:], key=lambda entry: entry[:2])

    def copy(self, mask, arrival, device):
        chunk = flip_mask(self.position, mask)
        return pltpu.make_async_remote_copy(
            src_ref=self.buffer.at[chunk],
            dst_ref=self.buffer.at[chunk],
            send_sem=self.send_sems.at[arrival],
            recv_sem=self.recv_sems.at[arrival],
            device_id=device,
            device_id_type=pl.DeviceIdType.MESH,
        )

    def forward(self, mask, after=-1):
        for level in self.levels[after + 1 :]:
            for step, device in level.items():
                self.sends.append(self.copy(mask, mask | step, device))
                self.sends[-1].start()

    def arrive(self, mask, number):
        level = self.levels[number]
        step = [step for step in level if mask & sum_bits(level) == step][0]
        self.copy(mask, mask, level[step]).wait_recv()
        self.forward(mask, number)

    def finish(self):
        for copy in self.sends:
            copy.wait_send()


def sum_bits(level):
    union = 0
    for step in level:
        union |= step
    return union


class Total:
    def __init__(self, buffer, inbox, sems, position, levels):
        self.buffer, self.inbox, self.sems, self.position = buffer, inbox, sems, position
        self.levels, self.level, self.copies = levels, 0, []

    def start(self):
        self.copies = [
            pltpu.make_async_remote_copy(
                src_ref=self.buffer,
                dst_ref=self.inbox.at[step],
                send_sem=self.sems.at[0, step],
                recv_sem=self.sems.at[1, step],
                device_id=device,
                device_id_type=pl.DeviceIdType.MESH,
            )
            for step, device in self.levels[self.level].items()
        ]
        for copy in self.copies:
            copy.start()

    def advance(self):
        if self.level == len(self.levels):
            return
        for copy in self.copies:
            copy.wait()
        terms = {0: self.buffer[...]}
        terms.update({step: self.inbox[step] for step in self.levels[self.level]})
        while len(terms) > 1:
            bit = highest_bit(max(terms))
            terms = {mask: terms[mask] + terms[mask | bit] for mask in terms if not mask & bit}
        self.buffer[...] = terms[0]
        self.level += 1
        if self.level < len(self.levels):
            self.start()


def highest_bit(number):
    bit = 1
    while bit * 2 <= number:
        bit *= 2
    return bit


def exchange_kernel(
    names,
    sizes,
    tensor_ref,
    b_ref,
    c_ref,
    normal_ref,
    product_ref,
    t_buf,
    b_buf,
    c_buf,
    n_buf,
    gram_b,
    gram_c,
    b_in,
    c_in,
    pj_in,
    pk_in,
    c_split,
    b_flat,
    p_buf,
    t_sem,
    b_send,
    b_recv,
    c_send,
    c_recv,
    n_send,
    n_recv,
    gb_sem,
    gc_sem,
    pj_sem,
    pk_sem,
    own_sem,
):
    slab_rows = tensor_ref.shape[0]
    width = b_ref.shape[1]
    at = {name: lax.axis_index(name) for name in names}

    def partner(name, mask):
        return tuple(flip_mask(at[n], mask) if n == name else at[n] for n in names)

    def fetch(i):
        return pltpu.make_async_copy(tensor_ref.at[i], t_buf.at[i], t_sem.at[i])

    def levels_of(name, unit, direct):
        bits = bits_of(sizes[name])
        groups = [bits] if direct else [[bit] for bit in bits]
        return [
            {mask * unit: partner(name, mask) for mask in combinations_of(group)}
            for group in groups
        ]

    ia_levels = levels_of("ia", 1, direct_ia)
    c_levels = levels_of("ja", sizes["ia"], direct_ja) + ia_levels
    b_levels = levels_of("ka", sizes["ia"], direct_ka) + ia_levels
    n_levels = levels_of("ia", 1, direct_n)
    reach = {}
    for name in names:
        direct = {"ia": direct_ia or direct_n, "ja": True, "ka": direct_ka or direct_sums}[name]
        for level in levels_of(name, 1, direct):
            reach.update({(name, mask): device for mask, device in level.items()})
    partners = list(reach.values())
    barrier = pltpu.get_barrier_semaphore()
    for device in partners:
        pl.semaphore_signal(barrier, inc=1, device_id=device, device_id_type=pl.DeviceIdType.MESH)

    c_at = at["ja"] * sizes["ia"] + at["ia"]
    b_at = at["ka"] * sizes["ia"] + at["ia"]
    own_c = pltpu.make_async_copy(c_ref, c_buf.at[c_at], own_sem.at[0])
    own_b = pltpu.make_async_copy(b_ref, b_buf.at[b_at], own_sem.at[1])
    own_c.start()
    own_b.start()
    for i in range(slab_rows):
        fetch(i).start()
    own_c.wait()
    own_b.wait()
    pl.semaphore_wait(barrier, len(partners))

    c_all = Gather(c_buf, c_send, c_recv, c_at, c_levels)
    b_all = Gather(b_buf, b_send, b_recv, b_at, b_levels)
    c_all.forward(0)
    b_all.forward(0)
    arrivals = [entry + (c_all,) for entry in c_all.order] + [entry + (b_all,) for entry in b_all.order]
    for _, number, mask, gather in sorted(arrivals, key=lambda entry: entry[:2]):
        gather.arrive(mask, number)

    deep = c_buf.shape[0] * c_buf.shape[1]
    whole_c = c_buf[...].reshape(deep, width)
    high = whole_c.astype(jnp.bfloat16)
    c_split[:deep] = high
    c_split[deep : 2 * deep] = (whole_c - high.astype(jnp.float32)).astype(jnp.bfloat16)
    c_split[2 * deep :] = high
    gram_c[...] = exact_dot(whole_c, whole_c, ((0,), (0,)))

    slab = width // sizes["ia"]
    rows = pl.ds(pl.multiple_of(at["ia"] * slab, slab), slab)

    gram_sum_c = Total(gram_c.at[rows], c_in, gc_sem, at["ka"], levels_of("ka", 1, direct_sums))
    gram_sum_b = Total(gram_b.at[rows], b_in, gb_sem, at["ja"], levels_of("ja", 1, direct_sums))
    gram_sum_c.start()
    whole_b = b_buf[...].reshape(b_buf.shape[0] * b_buf.shape[1], width)
    b_flat[...] = whole_b
    gram_b[...] = exact_dot(whole_b, whole_b, ((0,), (0,)))
    gram_sum_b.start()

    def rows_of_product(first, last):
        def one(i, carry):
            fetch(i).wait()
            block = t_buf[i]
            block_high = block.astype(jnp.bfloat16)
            block_low = (block - block_high.astype(jnp.float32)).astype(jnp.bfloat16)
            section = jnp.dot(
                jnp.concatenate([block_low, block_high, block_high], axis=1),
                c_split[...],
                preferred_element_type=jnp.float32,
            )
            p_buf[pl.ds(i, 1), :] = jnp.sum(section * b_flat[...], axis=0, keepdims=True)
            return carry

        lax.fori_loop(first, last, one, 0)

    parts = max(len(gram_sum_b.levels), len(gram_sum_c.levels))
    cuts = [slab_rows * p // parts for p in range(parts + 1)]
    for part in range(parts):
        rows_of_product(cuts[part], cuts[part + 1])
        gram_sum_c.advance()
        gram_sum_b.advance()

    n_buf[at["ia"]] = gram_b[rows, :] * gram_c[rows, :]
    n_all = Gather(n_buf, n_send, n_recv, at["ia"], n_levels)
    n_all.forward(0)
    sum_ja = Total(p_buf, pj_in, pj_sem, at["ja"], levels_of("ja", 1, direct_sums))
    sum_ka = Total(p_buf, pk_in, pk_sem, at["ka"], levels_of("ka", 1, direct_sums))
    sum_ja.start()
    while sum_ja.level < len(sum_ja.levels):
        sum_ja.advance()
    sum_ka.start()
    for _, number, mask in n_all.order:
        n_all.arrive(mask, number)
    normal_ref[...] = n_buf[...].reshape(width, width)
    while sum_ka.level < len(sum_ka.levels):
        sum_ka.advance()
    product_ref[...] = p_buf[...]
    n_all.finish()
    b_all.finish()
    c_all.finish()


def inverse_of(matrix):
    size = matrix.shape[0]
    count = size // tile_rows
    blocks = [matrix[tile_rows * i : tile_rows * (i + 1), :] for i in range(count)]
    lane = lax.broadcasted_iota(jnp.int32, (tile_rows, size), 1)
    row = lax.broadcasted_iota(jnp.int32, (tile_rows, size), 0)
    full = (tile_rows, size)
    for b in range(count):
        start = tile_rows * b
        inside = (lane >= start) & (lane < start + tile_rows)
        own = [
            jnp.broadcast_to(blocks[b][:, start + j : start + j + 1], full)
            for j in range(tile_rows)
        ]
        panel = jnp.where(inside, jnp.where(lane - start == row, 1.0, 0.0), blocks[b])
        for j in range(tile_rows):
            scale = 1.0 / jnp.broadcast_to(own[j][j : j + 1, :], full)
            here = row == j
            factor = jnp.where(here, 0.0, own[j])
            for c in range(j + 1, tile_rows):
                line = jnp.broadcast_to(own[c][j : j + 1, :], full) * scale
                own[c] = jnp.where(here, line, own[c] - factor * line)
            line = jnp.broadcast_to(panel[j : j + 1, :], full) * scale
            panel = jnp.where(here, line, panel - factor * line)
        lines = [jnp.broadcast_to(panel[j : j + 1, :], full) for j in range(tile_rows)]
        for i in range(count):
            if i == b:
                continue
            new = jnp.where(inside, 0.0, blocks[i])
            for j in range(tile_rows):
                new = new - jnp.broadcast_to(blocks[i][:, start + j : start + j + 1], full) * lines[j]
            blocks[i] = new
        blocks[b] = panel
    return jnp.concatenate(blocks, axis=0)


def solve_kernel(normal_ref, product_ref, out_ref):
    half = normal_ref.shape[0] // 2
    plain, turned = ((1,), (0,)), ((1,), (1,))
    corner = inverse_of(normal_ref[:half, :half])
    below = normal_ref[half:, :half]
    weight = exact_dot(below, corner, plain)
    rest = inverse_of(normal_ref[half:, half:] - exact_dot(weight, below, turned))
    left, right = product_ref[:, :half], product_ref[:, half:]
    second = exact_dot(right - exact_dot(left, weight, turned), rest, plain)
    out_ref[:, half:] = second
    out_ref[:, :half] = exact_dot(left - exact_dot(second, below, plain), corner, plain)


def shards(names, sizes, tensor, factor_b, factor_c):
    slab_rows, mode_two, mode_three = tensor.shape
    width = factor_b.shape[1]
    b_chunks, c_chunks = sizes["ka"] * sizes["ia"], sizes["ja"] * sizes["ia"]
    slab = width // sizes["ia"]
    f32, bf16 = jnp.float32, jnp.bfloat16
    vmem = pl.BlockSpec(memory_space=pltpu.VMEM)
    dma = pltpu.SemaphoreType.DMA
    normal, product = pl.pallas_call(
        functools.partial(exchange_kernel, names, sizes),
        out_shape=(
            jax.ShapeDtypeStruct((width, width), f32),
            jax.ShapeDtypeStruct((slab_rows, width), f32),
        ),
        in_specs=[pl.BlockSpec(memory_space=pltpu.HBM)] * 3,
        out_specs=(vmem, vmem),
        scratch_shapes=[
            pltpu.VMEM(tensor.shape, f32),
            pltpu.VMEM((b_chunks,) + factor_b.shape, f32),
            pltpu.VMEM((c_chunks,) + factor_c.shape, f32),
            pltpu.VMEM((sizes["ia"], slab, width), f32),
            pltpu.VMEM((width, width), f32),
            pltpu.VMEM((width, width), f32),
            pltpu.VMEM((sizes["ja"], slab, width), f32),
            pltpu.VMEM((sizes["ka"], slab, width), f32),
            pltpu.VMEM((sizes["ja"], slab_rows, width), f32),
            pltpu.VMEM((sizes["ka"], slab_rows, width), f32),
            pltpu.VMEM((3 * mode_three, width), bf16),
            pltpu.VMEM((mode_two, width), f32),
            pltpu.VMEM((slab_rows, width), f32),
            dma((slab_rows,)),
            dma((b_chunks,)),
            dma((b_chunks,)),
            dma((c_chunks,)),
            dma((c_chunks,)),
            dma((sizes["ia"],)),
            dma((sizes["ia"],)),
            dma((2, sizes["ja"])),
            dma((2, sizes["ka"])),
            dma((2, sizes["ja"])),
            dma((2, sizes["ka"])),
            dma((2,)),
        ],
        compiler_params=pltpu.CompilerParams(
            collective_id=0, has_side_effects=True, vmem_limit_bytes=62 * 2**20
        ),
        name="exchange",
    )(tensor, factor_b, factor_c)
    return pl.pallas_call(
        solve_kernel,
        out_shape=jax.ShapeDtypeStruct((slab_rows, width), f32),
        in_specs=[vmem, vmem],
        out_specs=vmem,
        compiler_params=pltpu.CompilerParams(vmem_limit_bytes=16 * 2**20),
        name="solve",
    )(normal, product)


def solution(mesh):
    names = tuple(mesh.axis_names)
    sizes = {name: mesh.shape[name] for name in names}
    return jax.shard_map(
        functools.partial(shards, names, sizes),
        mesh=mesh,
        in_specs=(P("ia", "ja", "ka"), P(("ja", "ka", "ia"), None), P(("ka", "ja", "ia"), None)),
        out_specs=P("ia", None),
        check_vma=False,
    )
```

```python
import functools

import jax
import jax.numpy as jnp
from jax import lax
from jax.experimental import pallas as pl
from jax.experimental.pallas import tpu as pltpu
from jax.sharding import PartitionSpec as P

exact_mode = lax.Precision.HIGHEST
tile_rows = 8
direct_ja, direct_ka, direct_ia, direct_n, direct_sums = True, True, False, True, True


def bits_of(count):
    found, bit = [], count // 2
    while bit >= 1:
        found.append(bit)
        bit //= 2
    return found


def flip(index, bit):
    return index + bit * (1 - 2 * ((index // bit) % 2))


def flip_mask(index, mask):
    bit = 1
    while bit <= mask:
        if mask & bit:
            index = flip(index, bit)
        bit *= 2
    return index


def exact_dot(a, b, dims):
    return lax.dot_general(
        a, b, (dims, ((), ())), precision=exact_mode, preferred_element_type=jnp.float32
    )


def combinations_of(bits):
    found = [0]
    for bit in bits:
        found += [mask | bit for mask in found]
    return found[1:]


class Gather:
    def __init__(self, buffer, send_sems, recv_sems, position, levels):
        self.buffer, self.send_sems, self.recv_sems = buffer, send_sems, recv_sems
        self.position, self.levels = position, levels
        self.sends = []
        self.order = [(0, -1, 0)]
        for number, level in enumerate(levels):
            self.order += [
                (depth + 1, number, mask | step)
                for depth, _, mask in self.order
                for step in level
            ]
        self.order = sorted(self.order[1:], key=lambda entry: entry[:2])

    def copy(self, mask, arrival, device):
        chunk = flip_mask(self.position, mask)
        return pltpu.make_async_remote_copy(
            src_ref=self.buffer.at[chunk],
            dst_ref=self.buffer.at[chunk],
            send_sem=self.send_sems.at[arrival],
            recv_sem=self.recv_sems.at[arrival],
            device_id=device,
            device_id_type=pl.DeviceIdType.MESH,
        )

    def forward(self, mask, after=-1):
        for level in self.levels[after + 1 :]:
            for step, device in level.items():
                self.sends.append(self.copy(mask, mask | step, device))
                self.sends[-1].start()

    def arrive(self, mask, number):
        level = self.levels[number]
        step = [step for step in level if mask & sum_bits(level) == step][0]
        self.copy(mask, mask, level[step]).wait_recv()
        self.forward(mask, number)

    def finish(self):
        for copy in self.sends:
            copy.wait_send()


def sum_bits(level):
    union = 0
    for step in level:
        union |= step
    return union


class Total:
    def __init__(self, buffer, inbox, sems, position, levels):
        self.buffer, self.inbox, self.sems, self.position = buffer, inbox, sems, position
        self.levels, self.level, self.copies = levels, 0, []

    def start(self):
        self.copies = [
            pltpu.make_async_remote_copy(
                src_ref=self.buffer,
                dst_ref=self.inbox.at[step],
                send_sem=self.sems.at[0, step],
                recv_sem=self.sems.at[1, step],
                device_id=device,
                device_id_type=pl.DeviceIdType.MESH,
            )
            for step, device in self.levels[self.level].items()
        ]
        for copy in self.copies:
            copy.start()

    def advance(self):
        if self.level == len(self.levels):
            return
        for copy in self.copies:
            copy.wait()
        terms = {0: self.buffer[...]}
        terms.update({step: self.inbox[step] for step in self.levels[self.level]})
        while len(terms) > 1:
            bit = highest_bit(max(terms))
            terms = {mask: terms[mask] + terms[mask | bit] for mask in terms if not mask & bit}
        self.buffer[...] = terms[0]
        self.level += 1
        if self.level < len(self.levels):
            self.start()


def highest_bit(number):
    bit = 1
    while bit * 2 <= number:
        bit *= 2
    return bit


def exchange_kernel(
    names,
    sizes,
    tensor_ref,
    b_ref,
    c_ref,
    normal_ref,
    product_ref,
    t_buf,
    b_buf,
    c_buf,
    n_buf,
    gram_b,
    gram_c,
    b_in,
    c_in,
    pj_in,
    pk_in,
    c_split,
    b_flat,
    p_buf,
    t_sem,
    b_send,
    b_recv,
    c_send,
    c_recv,
    n_send,
    n_recv,
    gb_sem,
    gc_sem,
    pj_sem,
    pk_sem,
    own_sem,
):
    slab_rows = tensor_ref.shape[0]
    width = b_ref.shape[1]
    at = {name: lax.axis_index(name) for name in names}

    def partner(name, mask):
        return tuple(flip_mask(at[n], mask) if n == name else at[n] for n in names)

    def fetch(i):
        return pltpu.make_async_copy(tensor_ref.at[i], t_buf.at[i], t_sem.at[i])

    def levels_of(name, unit, direct):
        bits = bits_of(sizes[name])
        groups = [bits] if direct else [[bit] for bit in bits]
        return [
            {mask * unit: partner(name, mask) for mask in combinations_of(group)}
            for group in groups
        ]

    ia_levels = levels_of("ia", 1, direct_ia)
    c_levels = levels_of("ja", sizes["ia"], direct_ja) + ia_levels
    b_levels = levels_of("ka", sizes["ia"], direct_ka) + ia_levels
    n_levels = levels_of("ia", 1, direct_n)
    reach = {}
    for name in names:
        direct = {"ia": direct_ia or direct_n, "ja": True, "ka": direct_ka or direct_sums}[name]
        for level in levels_of(name, 1, direct):
            reach.update({(name, mask): device for mask, device in level.items()})
    partners = list(reach.values())
    barrier = pltpu.get_barrier_semaphore()
    for device in partners:
        pl.semaphore_signal(barrier, inc=1, device_id=device, device_id_type=pl.DeviceIdType.MESH)

    c_at = at["ja"] * sizes["ia"] + at["ia"]
    b_at = at["ka"] * sizes["ia"] + at["ia"]
    own_c = pltpu.make_async_copy(c_ref, c_buf.at[c_at], own_sem.at[0])
    own_b = pltpu.make_async_copy(b_ref, b_buf.at[b_at], own_sem.at[1])
    own_c.start()
    own_b.start()
    for i in range(slab_rows):
        fetch(i).start()
    own_c.wait()
    own_b.wait()
    pl.semaphore_wait(barrier, len(partners))

    c_all = Gather(c_buf, c_send, c_recv, c_at, c_levels)
    b_all = Gather(b_buf, b_send, b_recv, b_at, b_levels)
    c_all.forward(0)
    b_all.forward(0)
    late = max(depth for depth, _, _ in b_all.order)
    arrivals = [entry + (c_all,) for entry in c_all.order]
    arrivals += [entry + (b_all,) for entry in b_all.order if entry[0] < late]
    for _, number, mask, gather in sorted(arrivals, key=lambda entry: entry[:2]):
        gather.arrive(mask, number)

    deep = c_buf.shape[0] * c_buf.shape[1]
    whole_c = c_buf[...].reshape(deep, width)
    high = whole_c.astype(jnp.bfloat16)
    c_split[:deep] = high
    c_split[deep : 2 * deep] = (whole_c - high.astype(jnp.float32)).astype(jnp.bfloat16)
    c_split[2 * deep :] = high
    gram_c[...] = exact_dot(whole_c, whole_c, ((0,), (0,)))

    slab = width // sizes["ia"]
    rows = pl.ds(pl.multiple_of(at["ia"] * slab, slab), slab)

    gram_sum_c = Total(gram_c.at[rows], c_in, gc_sem, at["ka"], levels_of("ka", 1, direct_sums))
    gram_sum_b = Total(gram_b.at[rows], b_in, gb_sem, at["ja"], levels_of("ja", 1, direct_sums))
    gram_sum_c.start()
    for depth, number, mask in b_all.order:
        if depth == late:
            b_all.arrive(mask, number)
    whole_b = b_buf[...].reshape(b_buf.shape[0] * b_buf.shape[1], width)
    b_flat[...] = whole_b
    gram_b[...] = exact_dot(whole_b, whole_b, ((0,), (0,)))
    gram_sum_b.start()

    def rows_of_product(first, last):
        def one(i, carry):
            fetch(i).wait()
            block = t_buf[i]
            block_high = block.astype(jnp.bfloat16)
            block_low = (block - block_high.astype(jnp.float32)).astype(jnp.bfloat16)
            section = jnp.dot(
                jnp.concatenate([block_low, block_high, block_high], axis=1),
                c_split[...],
                preferred_element_type=jnp.float32,
            )
            p_buf[pl.ds(i, 1), :] = jnp.sum(section * b_flat[...], axis=0, keepdims=True)
            return carry

        lax.fori_loop(first, last, one, 0)

    parts = max(len(gram_sum_b.levels), len(gram_sum_c.levels))
    cuts = [slab_rows * p // parts for p in range(parts + 1)]
    for part in range(parts):
        rows_of_product(cuts[part], cuts[part + 1])
        gram_sum_c.advance()
        gram_sum_b.advance()

    n_buf[at["ia"]] = gram_b[rows, :] * gram_c[rows, :]
    n_all = Gather(n_buf, n_send, n_recv, at["ia"], n_levels)
    n_all.forward(0)
    sum_ja = Total(p_buf, pj_in, pj_sem, at["ja"], levels_of("ja", 1, direct_sums))
    sum_ka = Total(p_buf, pk_in, pk_sem, at["ka"], levels_of("ka", 1, direct_sums))
    sum_ja.start()
    while sum_ja.level < len(sum_ja.levels):
        sum_ja.advance()
    sum_ka.start()
    for _, number, mask in n_all.order:
        n_all.arrive(mask, number)
    normal_ref[...] = n_buf[...].reshape(width, width)
    while sum_ka.level < len(sum_ka.levels):
        sum_ka.advance()
    product_ref[...] = p_buf[...]
    n_all.finish()
    b_all.finish()
    c_all.finish()


def inverse_of(matrix):
    size = matrix.shape[0]
    count = size // tile_rows
    blocks = [matrix[tile_rows * i : tile_rows * (i + 1), :] for i in range(count)]
    lane = lax.broadcasted_iota(jnp.int32, (tile_rows, size), 1)
    row = lax.broadcasted_iota(jnp.int32, (tile_rows, size), 0)
    full = (tile_rows, size)
    for b in range(count):
        start = tile_rows * b
        inside = (lane >= start) & (lane < start + tile_rows)
        own = [
            jnp.broadcast_to(blocks[b][:, start + j : start + j + 1], full)
            for j in range(tile_rows)
        ]
        panel = jnp.where(inside, jnp.where(lane - start == row, 1.0, 0.0), blocks[b])
        for j in range(tile_rows):
            scale = 1.0 / jnp.broadcast_to(own[j][j : j + 1, :], full)
            here = row == j
            factor = jnp.where(here, 0.0, own[j])
            for c in range(j + 1, tile_rows):
                line = jnp.broadcast_to(own[c][j : j + 1, :], full) * scale
                own[c] = jnp.where(here, line, own[c] - factor * line)
            line = jnp.broadcast_to(panel[j : j + 1, :], full) * scale
            panel = jnp.where(here, line, panel - factor * line)
        lines = [jnp.broadcast_to(panel[j : j + 1, :], full) for j in range(tile_rows)]
        for i in range(count):
            if i == b:
                continue
            new = jnp.where(inside, 0.0, blocks[i])
            for j in range(tile_rows):
                new = new - jnp.broadcast_to(blocks[i][:, start + j : start + j + 1], full) * lines[j]
            blocks[i] = new
        blocks[b] = panel
    return jnp.concatenate(blocks, axis=0)


def solve_kernel(normal_ref, product_ref, out_ref):
    half = normal_ref.shape[0] // 2
    plain, turned = ((1,), (0,)), ((1,), (1,))
    corner = inverse_of(normal_ref[:half, :half])
    below = normal_ref[half:, :half]
    weight = exact_dot(below, corner, plain)
    rest = inverse_of(normal_ref[half:, half:] - exact_dot(weight, below, turned))
    left, right = product_ref[:, :half], product_ref[:, half:]
    second = exact_dot(right - exact_dot(left, weight, turned), rest, plain)
    out_ref[:, half:] = second
    out_ref[:, :half] = exact_dot(left - exact_dot(second, below, plain), corner, plain)


def shards(names, sizes, tensor, factor_b, factor_c):
    slab_rows, mode_two, mode_three = tensor.shape
    width = factor_b.shape[1]
    b_chunks, c_chunks = sizes["ka"] * sizes["ia"], sizes["ja"] * sizes["ia"]
    slab = width // sizes["ia"]
    f32, bf16 = jnp.float32, jnp.bfloat16
    vmem = pl.BlockSpec(memory_space=pltpu.VMEM)
    dma = pltpu.SemaphoreType.DMA
    normal, product = pl.pallas_call(
        functools.partial(exchange_kernel, names, sizes),
        out_shape=(
            jax.ShapeDtypeStruct((width, width), f32),
            jax.ShapeDtypeStruct((slab_rows, width), f32),
        ),
        in_specs=[pl.BlockSpec(memory_space=pltpu.HBM)] * 3,
        out_specs=(vmem, vmem),
        scratch_shapes=[
            pltpu.VMEM(tensor.shape, f32),
            pltpu.VMEM((b_chunks,) + factor_b.shape, f32),
            pltpu.VMEM((c_chunks,) + factor_c.shape, f32),
            pltpu.VMEM((sizes["ia"], slab, width), f32),
            pltpu.VMEM((width, width), f32),
            pltpu.VMEM((width, width), f32),
            pltpu.VMEM((sizes["ja"], slab, width), f32),
            pltpu.VMEM((sizes["ka"], slab, width), f32),
            pltpu.VMEM((sizes["ja"], slab_rows, width), f32),
            pltpu.VMEM((sizes["ka"], slab_rows, width), f32),
            pltpu.VMEM((3 * mode_three, width), bf16),
            pltpu.VMEM((mode_two, width), f32),
            pltpu.VMEM((slab_rows, width), f32),
            dma((slab_rows,)),
            dma((b_chunks,)),
            dma((b_chunks,)),
            dma((c_chunks,)),
            dma((c_chunks,)),
            dma((sizes["ia"],)),
            dma((sizes["ia"],)),
            dma((2, sizes["ja"])),
            dma((2, sizes["ka"])),
            dma((2, sizes["ja"])),
            dma((2, sizes["ka"])),
            dma((2,)),
        ],
        compiler_params=pltpu.CompilerParams(
            collective_id=0, has_side_effects=True, vmem_limit_bytes=62 * 2**20
        ),
        name="exchange",
    )(tensor, factor_b, factor_c)
    return pl.pallas_call(
        solve_kernel,
        out_shape=jax.ShapeDtypeStruct((slab_rows, width), f32),
        in_specs=[vmem, vmem],
        out_specs=vmem,
        compiler_params=pltpu.CompilerParams(vmem_limit_bytes=16 * 2**20),
        name="solve",
    )(normal, product)


def solution(mesh):
    names = tuple(mesh.axis_names)
    sizes = {name: mesh.shape[name] for name in names}
    return jax.shard_map(
        functools.partial(shards, names, sizes),
        mesh=mesh,
        in_specs=(P("ia", "ja", "ka"), P(("ja", "ka", "ia"), None), P(("ka", "ja", "ia"), None)),
        out_specs=P("ia", None),
        check_vma=False,
    )
```

```python
import functools

import jax
import jax.numpy as jnp
from jax import lax
from jax.experimental import pallas as pl
from jax.experimental.pallas import tpu as pltpu
from jax.sharding import PartitionSpec as P

exact_mode = lax.Precision.HIGHEST
tile_rows = 8
direct_ja, direct_ka, direct_ia, direct_n, direct_sums = True, True, False, True, True


def bits_of(count):
    found, bit = [], count // 2
    while bit >= 1:
        found.append(bit)
        bit //= 2
    return found


def flip(index, bit):
    return index + bit * (1 - 2 * ((index // bit) % 2))


def flip_mask(index, mask):
    bit = 1
    while bit <= mask:
        if mask & bit:
            index = flip(index, bit)
        bit *= 2
    return index


def exact_dot(a, b, dims):
    return lax.dot_general(
        a, b, (dims, ((), ())), precision=exact_mode, preferred_element_type=jnp.float32
    )


def combinations_of(bits):
    found = [0]
    for bit in bits:
        found += [mask | bit for mask in found]
    return found[1:]


class Gather:
    def __init__(self, buffer, send_sems, recv_sems, position, levels):
        self.buffer, self.send_sems, self.recv_sems = buffer, send_sems, recv_sems
        self.position, self.levels = position, levels
        self.sends = []
        self.order = [(0, -1, 0)]
        for number, level in enumerate(levels):
            self.order += [
                (depth + 1, number, mask | step)
                for depth, _, mask in self.order
                for step in level
            ]
        self.order = sorted(self.order[1:], key=lambda entry: entry[:2])

    def copy(self, mask, arrival, device):
        chunk = flip_mask(self.position, mask)
        return pltpu.make_async_remote_copy(
            src_ref=self.buffer.at[chunk],
            dst_ref=self.buffer.at[chunk],
            send_sem=self.send_sems.at[arrival],
            recv_sem=self.recv_sems.at[arrival],
            device_id=device,
            device_id_type=pl.DeviceIdType.MESH,
        )

    def forward(self, mask, after=-1):
        for level in self.levels[after + 1 :]:
            for step, device in level.items():
                self.sends.append(self.copy(mask, mask | step, device))
                self.sends[-1].start()

    def arrive(self, mask, number):
        level = self.levels[number]
        step = [step for step in level if mask & sum_bits(level) == step][0]
        self.copy(mask, mask, level[step]).wait_recv()
        self.forward(mask, number)

    def finish(self):
        for copy in self.sends:
            copy.wait_send()


def sum_bits(level):
    union = 0
    for step in level:
        union |= step
    return union


class Total:
    def __init__(self, buffer, inbox, sems, position, levels):
        self.buffer, self.inbox, self.sems, self.position = buffer, inbox, sems, position
        self.levels, self.level, self.copies = levels, 0, []

    def start(self):
        self.copies = [
            pltpu.make_async_remote_copy(
                src_ref=self.buffer,
                dst_ref=self.inbox.at[step],
                send_sem=self.sems.at[0, step],
                recv_sem=self.sems.at[1, step],
                device_id=device,
                device_id_type=pl.DeviceIdType.MESH,
            )
            for step, device in self.levels[self.level].items()
        ]
        for copy in self.copies:
            copy.start()

    def advance(self):
        if self.level == len(self.levels):
            return
        for copy in self.copies:
            copy.wait()
        terms = {0: self.buffer[...]}
        terms.update({step: self.inbox[step] for step in self.levels[self.level]})
        while len(terms) > 1:
            bit = highest_bit(max(terms))
            terms = {mask: terms[mask] + terms[mask | bit] for mask in terms if not mask & bit}
        self.buffer[...] = terms[0]
        self.level += 1
        if self.level < len(self.levels):
            self.start()


def highest_bit(number):
    bit = 1
    while bit * 2 <= number:
        bit *= 2
    return bit


def exchange_kernel(
    names,
    sizes,
    tensor_ref,
    b_ref,
    c_ref,
    normal_ref,
    product_ref,
    t_buf,
    b_buf,
    c_buf,
    n_buf,
    gram_b,
    gram_c,
    b_in,
    c_in,
    pj_in,
    pk_in,
    c_split,
    b_flat,
    p_buf,
    t_sem,
    b_send,
    b_recv,
    c_send,
    c_recv,
    n_send,
    n_recv,
    gb_sem,
    gc_sem,
    pj_sem,
    pk_sem,
    own_sem,
):
    slab_rows = tensor_ref.shape[0]
    width = b_ref.shape[1]
    at = {name: lax.axis_index(name) for name in names}

    def partner(name, mask):
        return tuple(flip_mask(at[n], mask) if n == name else at[n] for n in names)

    def fetch(i):
        return pltpu.make_async_copy(tensor_ref.at[i], t_buf.at[i], t_sem.at[i])

    def levels_of(name, unit, direct):
        bits = bits_of(sizes[name])
        groups = [bits] if direct else [[bit] for bit in bits]
        return [
            {mask * unit: partner(name, mask) for mask in combinations_of(group)}
            for group in groups
        ]

    ia_levels = levels_of("ia", 1, direct_ia)
    c_levels = levels_of("ja", sizes["ia"], direct_ja) + ia_levels
    b_levels = levels_of("ka", sizes["ia"], direct_ka) + ia_levels
    n_levels = levels_of("ia", 1, direct_n)
    reach = {}
    for name in names:
        direct = {"ia": direct_ia or direct_n, "ja": True, "ka": direct_ka or direct_sums}[name]
        for level in levels_of(name, 1, direct):
            reach.update({(name, mask): device for mask, device in level.items()})
    partners = list(reach.values())
    barrier = pltpu.get_barrier_semaphore()
    for device in partners:
        pl.semaphore_signal(barrier, inc=1, device_id=device, device_id_type=pl.DeviceIdType.MESH)

    c_at = at["ja"] * sizes["ia"] + at["ia"]
    b_at = at["ka"] * sizes["ia"] + at["ia"]
    own_c = pltpu.make_async_copy(c_ref, c_buf.at[c_at], own_sem.at[0])
    own_b = pltpu.make_async_copy(b_ref, b_buf.at[b_at], own_sem.at[1])
    own_c.start()
    own_b.start()
    for i in range(slab_rows):
        fetch(i).start()
    own_c.wait()
    own_b.wait()
    pl.semaphore_wait(barrier, len(partners))

    c_all = Gather(c_buf, c_send, c_recv, c_at, c_levels)
    b_all = Gather(b_buf, b_send, b_recv, b_at, b_levels)
    c_all.forward(0)
    b_all.forward(0)
    late = max(depth for depth, _, _ in b_all.order)
    arrivals = [entry + (c_all,) for entry in c_all.order]
    arrivals += [entry + (b_all,) for entry in b_all.order if entry[0] < late]
    for _, number, mask, gather in sorted(arrivals, key=lambda entry: entry[:2]):
        gather.arrive(mask, number)

    deep = c_buf.shape[0] * c_buf.shape[1]
    whole_c = c_buf[...].reshape(deep, width)
    high = whole_c.astype(jnp.bfloat16)
    c_split[:deep] = high
    c_split[deep : 2 * deep] = (whole_c - high.astype(jnp.float32)).astype(jnp.bfloat16)
    c_split[2 * deep :] = high
    gram_c[...] = exact_dot(whole_c, whole_c, ((0,), (0,)))

    slab = width // sizes["ia"]
    rows = pl.ds(pl.multiple_of(at["ia"] * slab, slab), slab)

    gram_sum_c = Total(gram_c.at[rows], c_in, gc_sem, at["ka"], levels_of("ka", 1, direct_sums))
    gram_sum_b = Total(gram_b.at[rows], b_in, gb_sem, at["ja"], levels_of("ja", 1, direct_sums))
    gram_sum_c.start()
    for depth, number, mask in b_all.order:
        if depth == late:
            b_all.arrive(mask, number)
    whole_b = b_buf[...].reshape(b_buf.shape[0] * b_buf.shape[1], width)
    b_flat[...] = whole_b
    gram_b[...] = exact_dot(whole_b, whole_b, ((0,), (0,)))
    gram_sum_b.start()

    def rows_of_product(first, last):
        def one(i, carry):
            fetch(i).wait()
            block = t_buf[i]
            block_high = block.astype(jnp.bfloat16)
            block_low = (block - block_high.astype(jnp.float32)).astype(jnp.bfloat16)
            section = jnp.dot(
                jnp.concatenate([block_low, block_high, block_high], axis=1),
                c_split[...],
                preferred_element_type=jnp.float32,
            )
            p_buf[pl.ds(i, 1), :] = jnp.sum(section * b_flat[...], axis=0, keepdims=True)
            return carry

        lax.fori_loop(first, last, one, 0)

    parts = max(len(gram_sum_b.levels), len(gram_sum_c.levels))
    cuts = [slab_rows * p // parts for p in range(parts + 1)]
    for part in range(parts):
        rows_of_product(cuts[part], cuts[part + 1])
        gram_sum_c.advance()
        gram_sum_b.advance()

    n_buf[at["ia"]] = gram_b[rows, :] * gram_c[rows, :]
    n_all = Gather(n_buf, n_send, n_recv, at["ia"], n_levels)
    n_all.forward(0)
    sum_ja = Total(p_buf, pj_in, pj_sem, at["ja"], levels_of("ja", 1, direct_sums))
    sum_ka = Total(p_buf, pk_in, pk_sem, at["ka"], levels_of("ka", 1, direct_sums))
    sum_ja.start()
    while sum_ja.level < len(sum_ja.levels):
        sum_ja.advance()
    sum_ka.start()
    for _, number, mask in n_all.order:
        n_all.arrive(mask, number)
    normal_ref[...] = n_buf[...].reshape(width, width)
    while sum_ka.level < len(sum_ka.levels):
        sum_ka.advance()
    product_ref[...] = p_buf[...]
    n_all.finish()
    b_all.finish()
    c_all.finish()


def inverse_of(matrix):
    size = matrix.shape[0]
    count = size // tile_rows
    blocks = [matrix[tile_rows * i : tile_rows * (i + 1), :] for i in range(count)]
    lane = lax.broadcasted_iota(jnp.int32, (tile_rows, size), 1)
    row = lax.broadcasted_iota(jnp.int32, (tile_rows, size), 0)
    full = (tile_rows, size)
    for b in range(count):
        start = tile_rows * b
        inside = (lane >= start) & (lane < start + tile_rows)
        own = [
            jnp.broadcast_to(blocks[b][:, start + j : start + j + 1], full)
            for j in range(tile_rows)
        ]
        panel = jnp.where(inside, jnp.where(lane - start == row, 1.0, 0.0), blocks[b])
        for j in range(tile_rows):
            scale = 1.0 / jnp.broadcast_to(own[j][j : j + 1, :], full)
            here = row == j
            factor = jnp.where(here, 0.0, own[j])
            for c in range(j + 1, tile_rows):
                line = jnp.broadcast_to(own[c][j : j + 1, :], full) * scale
                own[c] = jnp.where(here, line, own[c] - factor * line)
            line = jnp.broadcast_to(panel[j : j + 1, :], full) * scale
            panel = jnp.where(here, line, panel - factor * line)
        lines = [jnp.broadcast_to(panel[j : j + 1, :], full) for j in range(tile_rows)]
        for i in range(count):
            if i == b:
                continue
            new = jnp.where(inside, 0.0, blocks[i])
            for j in range(tile_rows):
                new = new - jnp.broadcast_to(blocks[i][:, start + j : start + j + 1], full) * lines[j]
            blocks[i] = new
        blocks[b] = panel
    return jnp.concatenate(blocks, axis=0)


def solve_kernel(normal_ref, product_ref, out_ref):
    half = normal_ref.shape[0] // 2
    plain, turned = ((1,), (0,)), ((1,), (1,))
    corner = inverse_of(normal_ref[:half, :half])
    below = normal_ref[half:, :half]
    weight = exact_dot(below, corner, plain)
    rest = inverse_of(normal_ref[half:, half:] - exact_dot(weight, below, turned))
    left, right = product_ref[:, :half], product_ref[:, half:]
    second = exact_dot(right - exact_dot(left, weight, turned), rest, plain)
    out_ref[:, half:] = second
    out_ref[:, :half] = exact_dot(left - exact_dot(second, below, plain), corner, plain)


def shards(names, sizes, tensor, factor_b, factor_c):
    slab_rows, mode_two, mode_three = tensor.shape
    width = factor_b.shape[1]
    b_chunks, c_chunks = sizes["ka"] * sizes["ia"], sizes["ja"] * sizes["ia"]
    slab = width // sizes["ia"]
    f32, bf16 = jnp.float32, jnp.bfloat16
    vmem = pl.BlockSpec(memory_space=pltpu.VMEM)
    dma = pltpu.SemaphoreType.DMA
    normal, product = pl.pallas_call(
        functools.partial(exchange_kernel, names, sizes),
        out_shape=(
            jax.ShapeDtypeStruct((width, width), f32),
            jax.ShapeDtypeStruct((slab_rows, width), f32),
        ),
        in_specs=[pl.BlockSpec(memory_space=pltpu.HBM)] * 3,
        out_specs=(vmem, vmem),
        scratch_shapes=[
            pltpu.VMEM(tensor.shape, f32),
            pltpu.VMEM((b_chunks,) + factor_b.shape, f32),
            pltpu.VMEM((c_chunks,) + factor_c.shape, f32),
            pltpu.VMEM((sizes["ia"], slab, width), f32),
            pltpu.VMEM((width, width), f32),
            pltpu.VMEM((width, width), f32),
            pltpu.VMEM((sizes["ja"], slab, width), f32),
            pltpu.VMEM((sizes["ka"], slab, width), f32),
            pltpu.VMEM((sizes["ja"], slab_rows, width), f32),
            pltpu.VMEM((sizes["ka"], slab_rows, width), f32),
            pltpu.VMEM((3 * mode_three, width), bf16),
            pltpu.VMEM((mode_two, width), f32),
            pltpu.VMEM((slab_rows, width), f32),
            dma((slab_rows,)),
            dma((b_chunks,)),
            dma((b_chunks,)),
            dma((c_chunks,)),
            dma((c_chunks,)),
            dma((sizes["ia"],)),
            dma((sizes["ia"],)),
            dma((2, sizes["ja"])),
            dma((2, sizes["ka"])),
            dma((2, sizes["ja"])),
            dma((2, sizes["ka"])),
            dma((2,)),
        ],
        compiler_params=pltpu.CompilerParams(
            collective_id=0, has_side_effects=True, vmem_limit_bytes=54 * 2**20
        ),
        name="exchange",
    )(tensor, factor_b, factor_c)
    return pl.pallas_call(
        solve_kernel,
        out_shape=jax.ShapeDtypeStruct((slab_rows, width), f32),
        in_specs=[vmem, vmem],
        out_specs=vmem,
        compiler_params=pltpu.CompilerParams(vmem_limit_bytes=16 * 2**20),
        name="solve",
    )(normal, product)


def solution(mesh):
    names = tuple(mesh.axis_names)
    sizes = {name: mesh.shape[name] for name in names}
    return jax.shard_map(
        functools.partial(shards, names, sizes),
        mesh=mesh,
        in_specs=(P("ia", "ja", "ka"), P(("ja", "ka", "ia"), None), P(("ka", "ja", "ia"), None)),
        out_specs=P("ia", None),
        check_vma=False,
    )
```
